256 devices in a mesh: wide: 64 (over x, z, core), narrow: 4 (over y).
Axes of the slice: x: 4, y: 4, z: 8, core: 2. Of those that a mesh axis runs over, the one named last changes fastest.
Arguments:
- dosage: bfloat16 [262144, 4096], P(('wide', 'narrow')), may hold values from 0 to 2
- keep_rows: int32 [229376], P(('wide', 'narrow')), may hold values from 0 to 1023, as said below
- allele_counts: int32 [4096], replicated, may hold values from 157286 to 367000, as said below
- projection: bfloat16 [4096, 128], replicated, may hold values from -0.09375 to 0.09375
Outputs:
- scores: float32 [229376, 128], P(('wide', 'narrow'))
- loadings: float32 [4096, 128], P('narrow')
The draws below stay inside these ranges and needn't reach their ends.
Inputs may be any that keep to these rules, and one draw needn't show every extreme that they name: `keep_rows`: each block of 896 entries holds distinct local row numbers of one device's 1024 samples, ascending. `allele_counts`: totals over all 262144 genotyped samples, before outlier removal.
All inputs are finite; a program needn't handle non-finite values.
Results may differ from the reference program's by a relative error of at most 0.0075.
The reference program's roundings to bfloat16 on the way count: a program that leaves them out, or rounds other values in their place, can miss the bound.
Values sent between devices are 32-bit elements; how exact they have to be, the bound alone decides.
A program may use at most 64 MiB of HBM per device.

```python
import math
import jax
import jax.numpy as jnp
from jax import lax

SNPS = 4096
COMPONENTS = 128
ITERS = 2
SAMP_DEV = 1024
KEEP_DEV = 896
BLOCKS = 256
NARROW_BLOCKS = 4
SAMPLES = 262144
KEPT = 229376


def allele_draw(key):
    lowest = 3 * SAMPLES // 5
    highest = 7 * SAMPLES // 5
    counts_base = jax.random.randint(jax.random.fold_in(key, 11), (SNPS,), lowest, highest)
    first_slot = jax.random.randint(jax.random.fold_in(key, 12), (), 0, SNPS)
    shift_by = jax.random.randint(jax.random.fold_in(key, 13), (), 1, SNPS)
    second_slot = (first_slot + shift_by) % SNPS
    counts_base = counts_base.at[first_slot].set(lowest)
    counts_base = counts_base.at[second_slot].set(highest - 1)
    return counts_base.astype(jnp.int32)


def draw_allele_counts(key, part):
    return allele_draw(key)


def draw_dosage(key, part):
    counts = allele_draw(key)
    frequency = counts.astype(jnp.float32) / (2.0 * SAMPLES)
    noise_field = jnp.clip(0.5 * jax.random.normal(jax.random.fold_in(key, 22), (SAMPLES, SNPS), jnp.float32), -1.0, 1.0)
    block_index = jnp.arange(SAMPLES) // SAMP_DEV
    wide_pos = (block_index // NARROW_BLOCKS).astype(jnp.float32)
    narrow_pos = (block_index % NARROW_BLOCKS).astype(jnp.float32)
    wide_count = BLOCKS // NARROW_BLOCKS
    wide_frac = wide_pos / (wide_count - 1)
    narrow_frac = narrow_pos / (NARROW_BLOCKS - 1)
    power = (1.0 + wide_frac + narrow_frac) / 3.0
    amplitude = 0.6 * jnp.sqrt(power)
    values = 2.0 * frequency[None, :] + amplitude[:, None] * noise_field
    factors = 8
    sample_factors = jnp.clip(jax.random.normal(jax.random.fold_in(key, 41), (SAMPLES, factors), jnp.float32), -3.0, 3.0)
    snp_factors = jnp.clip(jax.random.normal(jax.random.fold_in(key, 42), (factors, SNPS), jnp.float32), -3.0, 3.0)
    for factor in range(factors):
        strength = 1.2 * 0.85 ** factor / math.sqrt(SNPS)
        values = values + sample_factors[:, factor][:, None] * (strength * snp_factors[factor])[None, :]
    return jnp.clip(values, 0.0, 2.0).astype(jnp.bfloat16)


def draw_keep_rows(key, part):
    block_keys = jax.random.split(jax.random.fold_in(key, 31), BLOCKS)

    def choose_rows(one_key):
        return jnp.sort(jax.random.permutation(one_key, SAMP_DEV)[:KEEP_DEV])
    return jax.vmap(choose_rows)(block_keys).reshape(KEPT).astype(jnp.int32)


def normal_values(own_key, dims, deviation, most, kind=jnp.bfloat16):
    return jnp.clip(deviation * jax.random.normal(own_key, dims, jnp.float32), -most, most).astype(kind)


def setup_inputs(seed: int = 0) -> dict:
    splits = jax.random.split(jax.random.key(seed), 5)
    dosage = draw_dosage(jax.random.fold_in(splits[4], 71), 0)
    keep_rows = draw_keep_rows(jax.random.fold_in(splits[4], 71), 0)
    allele_counts = draw_allele_counts(jax.random.fold_in(splits[4], 71), 0)
    projection = normal_values(splits[3], (SNPS, COMPONENTS), SNPS ** -0.5, 0.09375)
    return {"dosage": dosage, "keep_rows": keep_rows, "allele_counts": allele_counts, "projection": projection}


def standardize(dosage, keep_rows, allele_counts):
    frequency = allele_counts.astype(jnp.float32) / (2.0 * SAMPLES)
    center = 2.0 * frequency
    spread = jnp.sqrt(2.0 * frequency * (1.0 - frequency))
    blocks = dosage.reshape(BLOCKS, SAMP_DEV, SNPS)
    picks = keep_rows.reshape(BLOCKS, KEEP_DEV)

    def one_block(pair):
        block_rows, pick_rows = pair
        chosen = jnp.take(block_rows, pick_rows, axis=0)
        return ((chosen.astype(jnp.float32) - center) / spread).astype(jnp.bfloat16)
    return lax.map(one_block, (blocks, picks)).reshape(KEPT, SNPS)

def invert_factor(gram_matrix):
    lower_factor = jnp.linalg.cholesky(gram_matrix)
    unit_matrix = jnp.eye(gram_matrix.shape[0], dtype=jnp.float32)
    return jax.scipy.linalg.solve_triangular(lower_factor, unit_matrix, lower=True)

def reference(dosage, keep_rows, allele_counts, projection):
    standard = standardize(dosage, keep_rows, allele_counts)
    basis_bf = projection
    projected = None
    inverse = None
    loadings = None
    for iteration in range(ITERS):
        projected = jnp.dot(standard.astype(jnp.float32), basis_bf.astype(jnp.float32), preferred_element_type=jnp.float32).astype(jnp.bfloat16)
        gram_matrix = jnp.dot(projected.T.astype(jnp.float32), projected.astype(jnp.float32), preferred_element_type=jnp.float32)
        inverse = invert_factor(gram_matrix)
        partial_value = jnp.dot(standard.T.astype(jnp.float32), projected.astype(jnp.float32), preferred_element_type=jnp.float32)
        loadings = jnp.dot(partial_value, inverse.T, precision=lax.Precision.HIGHEST)
        basis_bf = loadings.astype(jnp.bfloat16)
    scores = jnp.dot(projected.astype(jnp.float32), inverse.T, precision=lax.Precision.HIGHEST) * math.sqrt(KEPT)
    return (scores, loadings)
```

```python
import functools
import itertools
import math

import jax
import jax.numpy as jnp
from jax import lax
from jax.experimental import pallas as pl
from jax.experimental.pallas import tpu as pltpu
from jax.sharding import PartitionSpec as P

X, Y, Z, C = 4, 4, 8, 2
LANES = 128
SNP_GROUP = 4 * LANES
ROW_CHUNK = 256
LANE_CHUNK = 1024
PIVOTS = 4
ITERS = 2
MESH = pl.DeviceIdType.MESH
HIGHEST = lax.Precision.HIGHEST
F32 = jnp.float32
BF16 = jnp.bfloat16


def device_at(x, y, z, c):
    return ((x * Z + z) * C + c, y)


def iota(shape, dim):
    return lax.broadcasted_iota(jnp.int32, shape, dim)


def dot_t(left, right, precision=None):
    return lax.dot_general(
        left, right, (((1,), (1,)), ((), ())), precision=precision, preferred_element_type=F32
    )


def eliminate(work, first, last):
    n = work.shape[0]
    row = iota((n, 1), 0)
    lane = iota((n, n), 1)
    lane1 = iota((1, n), 1)

    def panel(step, carry):
        k = step * PIVOTS
        whole = work[...]
        rows = [work[pl.ds(k + i, 1), :] for i in range(PIVOTS)]
        entry = {
            (i, l): jnp.sum(jnp.where(lane1 == k + l, rows[i], 0.0), axis=1, keepdims=True)
            for i in range(PIVOTS)
            for l in range(i, PIVOTS)
        }
        columns = [
            jnp.sum(jnp.where(lane == k + l, whole, 0.0), axis=1, keepdims=True)
            for l in range(PIVOTS)
        ]
        total = jnp.where((lane >= k) & (lane < k + PIVOTS) & (row >= k + PIVOTS), 0.0, whole)
        factors = []
        for j in range(PIVOTS):
            turn = 1.0 / entry[j, j]
            factor = jnp.where(row > k + j, columns[j] * turn, 0.0)
            factors.append(factor)
            own = jnp.where(lane1 == k + j, 1.0, rows[j])
            for l in range(j + 1, PIVOTS):
                columns[l] = columns[l] - factor * entry[j, l]
                less = entry[j, l] * turn
                rows[l] = jnp.where(lane1 == k + j, 0.0, rows[l]) - less * own
                for later in range(l, PIVOTS):
                    entry[l, later] = entry[l, later] - less * entry[j, later]
        for j in range(PIVOTS):
            own = jnp.where(lane1 == k + j, 1.0, rows[j])
            own = jnp.where((lane1 > k + j) & (lane1 < k + PIVOTS), 0.0, own)
            total = total - factors[j] * own
        work[...] = total
        for j in range(PIVOTS):
            work[pl.ds(k + j, 1), :] = rows[j]
        return carry

    lax.fori_loop(first, last, panel, 0)


def finish_inverse(work):
    n = work.shape[0]
    whole = work[...]
    row, lane = iota((n, n), 0), iota((n, n), 1)
    pivot = jnp.sum(jnp.where(row == lane, whole, 0.0), axis=1, keepdims=True)
    unit = jnp.where(lane < row, whole, jnp.where(lane == row, 1.0, 0.0))
    return unit * (1.0 / jnp.sqrt(pivot))


def kernel(
    samples_total, kept_total,
    dose_ref, keep_ref, counts_ref, sketch_ref,
    scores_ref, loads_ref,
    std, center, scale, mask, proj, proj_t, acc, gram, inverse,
    tot, rxc, own, rx1a, rx1b, rx2a, rx2b, zsrc, rxz, fin, fin2,
    g_src, g_core, g_half, g_rx, g_y, g_z, g_x, g_full,
    load_sem, send_sem, recv_sem,
):
    wide = lax.axis_index("wide")
    y = lax.axis_index("narrow")
    x, z, c = wide // (Z * C), lax.rem(wide // C, Z), lax.rem(wide, C)
    d = 1 - c
    xs = [lax.rem(x + k, X) for k in range(X)]
    ys = [lax.rem(y + k, Y) for k in range(Y)]
    zs = [lax.rem(z + k, Z) for k in range(Z)]
    core_peer = device_at(x, y, z, d)
    x_peer = [device_at(v, y, z, c) for v in xs]
    y_peer = [device_at(x, v, z, c) for v in ys]
    z_peer = [device_at(x, y, v, c) for v in zs]
    chunks = std.shape[0] // ROW_CHUNK
    snps = std.shape[1]

    def load(r):
        rows = pl.ds(r * ROW_CHUNK, ROW_CHUNK)
        return pltpu.make_async_copy(dose_ref.at[rows], std.at[rows], load_sem.at[r])

    for r in range(chunks):
        load(r).start()
    barrier = pltpu.get_barrier_semaphore()
    others = [core_peer] + x_peer[1:] + y_peer[1:] + z_peer[1:]
    for other in others:
        pl.semaphore_signal(barrier, inc=1, device_id=other, device_id_type=MESH)

    counter = itertools.count()
    sends = []

    def describe(src, dst, sem, peer):
        return pltpu.make_async_remote_copy(
            src_ref=src, dst_ref=dst, send_sem=send_sem.at[sem], recv_sem=recv_sem.at[sem],
            device_id=peer, device_id_type=MESH,
        )

    def push(src, dst, peer):
        copy = describe(src, dst, next(counter), peer)
        copy.start()
        sends.append(copy)
        return copy

    frequency = counts_ref[...].astype(F32) / (2.0 * samples_total)
    center[...] = 2.0 * frequency
    scale[...] = 1.0 / jnp.sqrt(2.0 * frequency * (1.0 - frequency))
    keep_count = keep_ref.shape[1]
    ones = jnp.ones((keep_count, LANES), BF16)

    def mark(r, carry):
        hits = iota((ROW_CHUNK, keep_count), 0) + r * ROW_CHUNK == keep_ref[...]
        mask[pl.ds(pl.multiple_of(r * ROW_CHUNK, ROW_CHUNK), ROW_CHUNK), :] = jnp.dot(
            jnp.where(hits, 1.0, 0.0).astype(BF16), ones, preferred_element_type=F32
        )
        return carry

    lax.fori_loop(0, chunks, mark, 0)

    def keep_projection(r, value):
        rows = pl.ds(pl.multiple_of(r * ROW_CHUNK, ROW_CHUNK), ROW_CHUNK)
        value = value.astype(BF16).astype(F32) * mask[rows, :]
        proj[rows, :] = value.astype(BF16)
        proj_t[:, rows] = value.T.astype(BF16)

    def first_projection(r, carry):
        load(r).wait()
        rows = pl.ds(pl.multiple_of(r * ROW_CHUNK, ROW_CHUNK), ROW_CHUNK)
        value = jnp.zeros((ROW_CHUNK, LANES), F32)
        for q in range(snps // LANE_CHUNK):
            lanes = pl.ds(q * LANE_CHUNK, LANE_CHUNK)
            part = ((std[rows, lanes].astype(F32) - center[:, lanes]) * scale[:, lanes]).astype(BF16)
            std[rows, lanes] = part
            value = value + jnp.dot(part, sketch_ref[lanes, :], preferred_element_type=F32)
        keep_projection(r, value)
        return carry

    lax.fori_loop(0, chunks, first_projection, 0)

    def group_lanes(yy, cc):
        return pl.ds(pl.multiple_of((yy * C + cc) * SNP_GROUP, SNP_GROUP), SNP_GROUP)

    def partial_group(yy, cc):
        value = jnp.dot(proj_t[...], std[:, group_lanes(yy, cc)], preferred_element_type=F32)
        for q in range(X):
            tot[yy, cc, q] = value[:, q * LANES:(q + 1) * LANES].reshape(8, 16, LANES)

    for it in range(ITERS):
        last = it + 1 == ITERS
        g_src[it] = dot_t(proj_t[...], proj_t[...]).reshape(C, X, 16, LANES)
        if it == 0:
            pl.semaphore_wait(barrier, len(others))
        gram_core = push(g_src.at[it, d], g_core.at[it], core_peer)

        core_sem = next(counter)
        for _ in range(Y - 1):
            next(counter)

        def core_copy(j, it=it, core_sem=core_sem):
            yy = lax.rem(y + 1 + j, Y)
            return describe(tot.at[yy, d], rxc.at[it, yy], core_sem + j, core_peer)

        def partial_other(j, carry):
            partial_group(lax.rem(y + 1 + j, Y), d)
            core_copy(j).start()
            return carry

        def partial_own(j, carry):
            partial_group(lax.rem(y + 1 + j, Y), c)
            return carry

        lax.fori_loop(0, Y, partial_other, 0)
        gram_core.wait_recv()
        g_half[it] = g_src[it, c] + g_core[it]
        gram_x = [push(g_half.at[it, xs[k]], g_rx.at[it, k - 1], x_peer[k]) for k in range(1, X)]
        lax.fori_loop(0, Y, partial_own, 0)
        for copy in gram_x:
            copy.wait_recv()
        g_y[it, y] = g_half[it, x] + g_rx[it, 0] + g_rx[it, 1] + g_rx[it, 2]
        gram_y = [push(g_y.at[it, y], g_y.at[it, y], y_peer[k]) for k in range(1, Y)]

        first_a, first_b = {}, {}
        for j in (1, 2, 3, 0):
            core_copy((j + 3) % 4).wait_recv()
            yy = ys[j]
            own[it, yy] = tot[yy, c] + rxc[it, yy]
            for k in range(1, X):
                first_a[j, k] = push(
                    own.at[it, yy, xs[k], pl.ds(0, 4)], rx1a.at[it, k - 1, yy], x_peer[k]
                )
            if j:
                for k in (1, 2, 3, 0):
                    first_b[k, j] = push(
                        own.at[it, yy, xs[k], pl.ds(4, 4)], rx1b.at[it, j - 1, xs[k]], y_peer[j]
                    )
        for copy in gram_y:
            copy.wait_recv()
        g_z[it, z] = (g_y[it, 0] + g_y[it, 1]) + (g_y[it, 2] + g_y[it, 3])
        gram_z = [push(g_z.at[it, z], g_z.at[it, z], z_peer[k]) for k in range(1, Z)]

        second_a, second_b = [], []
        for j in (1, 2, 3, 0):
            for k in range(1, X):
                first_a[j, k].wait_recv()
            own[it, ys[j], x, 0:4] = (
                own[it, ys[j], x, 0:4] + rx1a[it, 0, ys[j]] + rx1a[it, 1, ys[j]] + rx1a[it, 2, ys[j]]
            )
            if j:
                second_a.append(push(own.at[it, ys[j], x, pl.ds(0, 4)], rx2a.at[it, j - 1], y_peer[j]))
            for k in range(1, Y):
                first_b[j, k].wait_recv()
            own[it, y, xs[j], 4:8] = (
                own[it, y, xs[j], 4:8] + rx1b[it, 0, xs[j]] + rx1b[it, 1, xs[j]] + rx1b[it, 2, xs[j]]
            )
            if j:
                second_b.append(push(own.at[it, y, xs[j], pl.ds(4, 4)], rx2b.at[it, j - 1], x_peer[j]))
        for copy in gram_z:
            copy.wait_recv()
        value = g_z[it, 0]
        for k in range(1, Z):
            value = value + g_z[it, k]
        g_x[it, x] = value
        gram_x = [push(g_x.at[it, x], g_x.at[it, x], x_peer[k]) for k in range(1, X)]
        for copy in second_a + second_b:
            copy.wait_recv()
        zsrc[it, 0:4] = own[it, y, x, 0:4] + rx2a[it, 0] + rx2a[it, 1] + rx2a[it, 2]
        zsrc[it, 4:8] = own[it, y, x, 4:8] + rx2b[it, 0] + rx2b[it, 1] + rx2b[it, 2]
        third = [push(zsrc.at[it, zs[k]], rxz.at[it, k - 1], z_peer[k]) for k in range(1, Z)]
        for copy in gram_x:
            copy.wait_recv()
        g_full[it, c] = g_x[it]
        gram_core = push(g_full.at[it, c], g_full.at[it, c], core_peer)
        for copy in third:
            copy.wait_recv()
        value = zsrc[it, z]
        for k in range(1, Z):
            value = value + rxz[it, k - 1]
        if last:
            mine = fin2.at[c, x]
        else:
            mine = fin.at[y, c, x]
        mine[z] = value
        gather_z = [push(mine.at[z], mine.at[z], z_peer[k]) for k in range(1, Z)]
        gram_core.wait_recv()
        gram[...] = g_full[it].reshape(LANES, LANES)
        panels = LANES // PIVOTS
        eliminate(gram, 0, 12)
        for copy in gather_z:
            copy.wait_recv()
        if last:
            gather_x = [push(mine, mine, x_peer[k]) for k in range(1, X)]
            gather_c = [push(mine, mine, core_peer)]
            eliminate(gram, 12, 20)
            for k in range(1, X):
                gather_x[k - 1].wait_recv()
                block = fin2.at[c, xs[X - k]]
                gather_c.append(push(block, block, core_peer))
            eliminate(gram, 20, panels)
            inverse[...] = finish_inverse(gram)
            keep_column = jnp.broadcast_to(keep_ref[...].astype(F32), (LANES, keep_count)).T
            value = jnp.zeros((keep_count, LANES), F32)
            for q in range(std.shape[0] // LANES):
                hits = keep_column == (iota((keep_count, LANES), 1) + q * LANES).astype(F32)
                value = value + jnp.dot(
                    jnp.where(hits, 1.0, 0.0).astype(BF16), proj[q * LANES:(q + 1) * LANES, :],
                    preferred_element_type=F32,
                )
            scores_ref[...] = dot_t(value, inverse[...], HIGHEST) * math.sqrt(kept_total)
            for copy in gather_c:
                copy.wait_recv()
            for cc in range(C):
                for q in range(X):
                    value = jnp.dot(
                        inverse[...], fin2[cc, q].reshape(LANES, LANES), precision=HIGHEST,
                        preferred_element_type=F32,
                    )
                    loads_ref[(cc * X + q) * LANES:(cc * X + q + 1) * LANES, :] = value.T
        else:
            gather_x = [push(mine, mine, x_peer[k]) for k in range(1, X)]
            gather_y = [push(mine, mine, y_peer[k]) for k in range(1, Y)]
            gather_c = [push(mine, mine, core_peer)]
            eliminate(gram, 12, 20)
            corner_a, corner_b = {}, {}
            for j in range(1, Y):
                gather_y[j - 1].wait_recv()
                block = fin.at[ys[Y - j], c, x]
                for k in range(1, X):
                    corner_a[j, k] = push(block.at[pl.ds(0, 4)], block.at[pl.ds(0, 4)], x_peer[k])
                gather_x[j - 1].wait_recv()
                block2 = fin.at[y, c, xs[X - j]]
                for k in range(1, Y):
                    corner_b[j, k] = push(block2.at[pl.ds(4, 4)], block2.at[pl.ds(4, 4)], y_peer[k])
                gather_c.append(push(block, block, core_peer))
                gather_c.append(push(block2, block2, core_peer))
            eliminate(gram, 20, panels)
            inverse[...] = finish_inverse(gram)
            for j in range(1, Y):
                for k in range(1, X):
                    corner_a[j, k].wait_recv()
                    corner_b[k, j].wait_recv()
                    block = fin.at[ys[Y - j], c, xs[X - k]]
                    gather_c.append(push(block, block, core_peer))

            def apply_group(yy, cc):
                value = jnp.concatenate([fin[yy, cc, q].reshape(LANES, LANES) for q in range(X)], axis=1)
                value = jnp.dot(inverse[...], value, precision=HIGHEST, preferred_element_type=F32)
                return dot_t(std[:, group_lanes(yy, cc)], value.astype(BF16))

            def project_own(j, carry):
                acc[...] = acc[...] + apply_group(lax.rem(y + j, Y), c)
                return carry

            def project_other(j, carry):
                acc[...] = acc[...] + apply_group(lax.rem(y + j, Y), d)
                return carry

            acc[...] = jnp.zeros_like(acc)
            lax.fori_loop(0, Y, project_own, 0)
            for copy in gather_c:
                copy.wait_recv()
            lax.fori_loop(0, Y, project_other, 0)

            def keep_chunk(r, carry):
                rows = pl.ds(pl.multiple_of(r * ROW_CHUNK, ROW_CHUNK), ROW_CHUNK)
                keep_projection(r, acc[rows, :])
                return carry

            lax.fori_loop(0, chunks, keep_chunk, 0)
        for j in range(Y):
            core_copy(j).wait_send()
    for copy in sends:
        copy.wait_send()


def on_device(dosage, keep_rows, allele_counts, projection):
    groups = lax.axis_size("wide") * lax.axis_size("narrow")
    samples, snps = dosage.shape
    kept = keep_rows.shape[0]
    shares = snps // Y
    vmem = pl.BlockSpec(memory_space=pltpu.VMEM)
    piece = (4, 16, LANES)
    block = (8, 16, LANES)
    scratch = [
        ((samples, snps), BF16),
        ((1, snps), F32),
        ((1, snps), F32),
        ((samples, LANES), F32),
        ((samples, LANES), BF16),
        ((LANES, samples), BF16),
        ((samples, LANES), F32),
        ((LANES, LANES), F32),
        ((LANES, LANES), F32),
        ((Y, C, X) + block, F32),
        ((ITERS, Y, X) + block, F32),
        ((ITERS, Y, X) + block, F32),
        ((ITERS, X - 1, Y) + piece, F32),
        ((ITERS, Y - 1, X) + piece, F32),
        ((ITERS, Y - 1) + piece, F32),
        ((ITERS, X - 1) + piece, F32),
        ((ITERS,) + block, F32),
        ((ITERS, Z - 1, 16, LANES), F32),
        ((Y, C, X) + block, F32),
        ((C, X) + block, F32),
        ((ITERS, C, X, 16, LANES), F32),
        ((ITERS, X, 16, LANES), F32),
        ((ITERS, X, 16, LANES), F32),
        ((ITERS, X - 1, 16, LANES), F32),
        ((ITERS, Y, 16, LANES), F32),
        ((ITERS, Z, 16, LANES), F32),
        ((ITERS, X, 16, LANES), F32),
        ((ITERS, C, X, 16, LANES), F32),
    ]
    return pl.pallas_call(
        functools.partial(kernel, samples * groups, kept * groups),
        name="subspace",
        out_shape=(
            jax.ShapeDtypeStruct((kept, LANES), F32),
            jax.ShapeDtypeStruct((shares, LANES), F32),
        ),
        in_specs=[pl.BlockSpec(memory_space=pl.ANY), vmem, vmem, vmem],
        out_specs=(vmem, vmem),
        scratch_shapes=[pltpu.VMEM(shape, kind) for shape, kind in scratch]
        + [
            pltpu.SemaphoreType.DMA((samples // ROW_CHUNK,)),
            pltpu.SemaphoreType.DMA((200,)),
            pltpu.SemaphoreType.DMA((200,)),
        ],
        compiler_params=pltpu.CompilerParams(
            collective_id=0, has_side_effects=True, vmem_limit_bytes=56 * 2**20
        ),
        cost_estimate=pl.CostEstimate(flops=4_500_000_000, bytes_accessed=12_000_000, transcendentals=0),
    )(dosage, keep_rows.reshape(1, kept), allele_counts.reshape(1, snps), projection)


def solution(mesh):
    in_specs = (P(("wide", "narrow"), None), P(("wide", "narrow")), P(), P())
    out_specs = (P(("wide", "narrow"), None), P("narrow", None))
    return jax.shard_map(
        on_device, mesh=mesh, in_specs=in_specs, out_specs=out_specs, check_vma=False
    )
```

```python
import functools
import itertools
import math

import jax
import jax.numpy as jnp
from jax import lax
from jax.experimental import pallas as pl
from jax.experimental.pallas import tpu as pltpu
from jax.sharding import PartitionSpec as P

X, Y, Z, C = 4, 4, 8, 2
LANES = 128
SNP_GROUP = 4 * LANES
ROW_CHUNK = 256
HALF_ROWS = 512
LANE_CHUNK = 1024
PIVOTS = 4
ITERS = 2
PARTS = 2
MESH = pl.DeviceIdType.MESH
HIGHEST = lax.Precision.HIGHEST
F32 = jnp.float32
BF16 = jnp.bfloat16


def device_at(x, y, z, c):
    return ((x * Z + z) * C + c, y)


def iota(shape, dim):
    return lax.broadcasted_iota(jnp.int32, shape, dim)


def dot_t(left, right, precision=None):
    return lax.dot_general(
        left, right, (((1,), (1,)), ((), ())), precision=precision, preferred_element_type=F32
    )


def eliminate(work, first, last):
    n = work.shape[0]
    row = iota((n, 1), 0)
    lane = iota((n, n), 1)
    lane1 = iota((1, n), 1)

    def panel(step, carry):
        k = step * PIVOTS
        whole = work[...]
        rows = [work[pl.ds(k + i, 1), :] for i in range(PIVOTS)]
        entry = {
            (i, l): jnp.sum(jnp.where(lane1 == k + l, rows[i], 0.0), axis=1, keepdims=True)
            for i in range(PIVOTS)
            for l in range(i, PIVOTS)
        }
        columns = [
            jnp.sum(jnp.where(lane == k + l, whole, 0.0), axis=1, keepdims=True)
            for l in range(PIVOTS)
        ]
        total = jnp.where((lane >= k) & (lane < k + PIVOTS) & (row >= k + PIVOTS), 0.0, whole)
        factors = []
        for j in range(PIVOTS):
            turn = 1.0 / entry[j, j]
            factor = jnp.where(row > k + j, columns[j] * turn, 0.0)
            factors.append(factor)
            own = jnp.where(lane1 == k + j, 1.0, rows[j])
            for l in range(j + 1, PIVOTS):
                columns[l] = columns[l] - factor * entry[j, l]
                less = entry[j, l] * turn
                rows[l] = jnp.where(lane1 == k + j, 0.0, rows[l]) - less * own
                for later in range(l, PIVOTS):
                    entry[l, later] = entry[l, later] - less * entry[j, later]
        for j in range(PIVOTS):
            own = jnp.where(lane1 == k + j, 1.0, rows[j])
            own = jnp.where((lane1 > k + j) & (lane1 < k + PIVOTS), 0.0, own)
            total = total - factors[j] * own
        work[...] = total
        for j in range(PIVOTS):
            work[pl.ds(k + j, 1), :] = rows[j]
        return carry

    lax.fori_loop(first, last, panel, 0)


def finish_inverse(work):
    n = work.shape[0]
    whole = work[...]
    row, lane = iota((n, n), 0), iota((n, n), 1)
    pivot = jnp.sum(jnp.where(row == lane, whole, 0.0), axis=1, keepdims=True)
    unit = jnp.where(lane < row, whole, jnp.where(lane == row, 1.0, 0.0))
    return unit * (1.0 / jnp.sqrt(pivot))


def hand_on(scores_in, loads_in, scores_out, loads_out, scores, loads, sem):
    parts = []
    for source, held, target in ((scores_in, scores, scores_out), (loads_in, loads, loads_out)):
        size = source.shape[0] // PARTS
        for q in range(PARTS):
            rows, n = pl.ds(q * size, size), len(parts)
            parts.append((
                pltpu.make_async_copy(source.at[rows], held.at[rows], sem.at[n]),
                pltpu.make_async_copy(held.at[rows], target.at[rows], sem.at[n + 2 * PARTS]),
            ))
    for read, _ in parts:
        read.start()
    for read, write in parts:
        read.wait()
        write.start()
    for _, write in parts:
        write.wait()


def kernel(
    samples_total, root,
    dose_ref, keep_ref, counts_ref, sketch_ref,
    scores_ref, loads_ref,
    std, sketch, center, scale, mask, proj, proj_t, acc, gram, inverse, basis_t, scores, loads, kept_proj,
    tot, rxc, own, rx1a, rx1b, rx2a, rx2b, zsrc, rxz, fin, fin2,
    g_src, g_core, g_half, g_rx, g_y, g_z, g_x, g_full,
    load_sem, sketch_sem, out_sem, send_sem, recv_sem,
):
    wide = lax.axis_index("wide")
    y = lax.axis_index("narrow")
    x, z, c = wide // (Z * C), lax.rem(wide // C, Z), lax.rem(wide, C)
    d = 1 - c
    xs = [lax.rem(x + k, X) for k in range(X)]
    ys = [lax.rem(y + k, Y) for k in range(Y)]
    zs = [lax.rem(z + k, Z) for k in range(Z)]
    core_peer = device_at(x, y, z, d)
    x_peer = [device_at(v, y, z, c) for v in xs]
    y_peer = [device_at(x, v, z, c) for v in ys]
    z_peer = [device_at(x, y, v, c) for v in zs]
    chunks = std.shape[0] // ROW_CHUNK
    snps = std.shape[1]

    def load(r):
        rows = pl.ds(r * ROW_CHUNK, ROW_CHUNK)
        return pltpu.make_async_copy(dose_ref.at[rows], std.at[rows], load_sem.at[r])

    sketch_load = pltpu.make_async_copy(sketch_ref, sketch, sketch_sem)
    sketch_load.start()
    for r in range(chunks):
        load(r).start()
    barrier = pltpu.get_barrier_semaphore()
    others = [core_peer] + x_peer[1:] + y_peer[1:] + z_peer[1:]
    for other in others:
        pl.semaphore_signal(barrier, inc=1, device_id=other, device_id_type=MESH)

    counter = itertools.count()
    sends = []

    def describe(src, dst, sem, peer):
        return pltpu.make_async_remote_copy(
            src_ref=src, dst_ref=dst, send_sem=send_sem.at[sem], recv_sem=recv_sem.at[sem],
            device_id=peer, device_id_type=MESH,
        )

    def push(src, dst, peer):
        copy = describe(src, dst, next(counter), peer)
        copy.start()
        sends.append(copy)
        return copy

    frequency = counts_ref[...].astype(F32) / (2.0 * samples_total)
    center[...] = 2.0 * frequency
    scale[...] = 1.0 / jnp.sqrt(2.0 * frequency * (1.0 - frequency))
    keep_row = jnp.concatenate([keep_ref[q:q + 1, :] for q in range(keep_ref.shape[0])], axis=1)
    keep_count = keep_row.shape[1]
    ones = jnp.ones((keep_count, LANES), BF16)

    def mark(r, carry):
        hits = iota((ROW_CHUNK, keep_count), 0) + r * ROW_CHUNK == keep_row
        mask[pl.ds(pl.multiple_of(r * ROW_CHUNK, ROW_CHUNK), ROW_CHUNK), :] = jnp.dot(
            jnp.where(hits, 1.0, 0.0).astype(BF16), ones, preferred_element_type=F32
        )
        return carry

    lax.fori_loop(0, chunks, mark, 0)

    def keep_projection(r, value):
        rows = pl.ds(pl.multiple_of(r * ROW_CHUNK, ROW_CHUNK), ROW_CHUNK)
        value = value.astype(BF16).astype(F32) * mask[rows, :]
        proj[rows, :] = value.astype(BF16)
        proj_t[:, rows] = value.T.astype(BF16)

    def first_projection(r, carry):
        load(r).wait()
        rows = pl.ds(pl.multiple_of(r * ROW_CHUNK, ROW_CHUNK), ROW_CHUNK)
        value = jnp.zeros((ROW_CHUNK, LANES), F32)
        for q in range(snps // LANE_CHUNK):
            lanes = pl.ds(q * LANE_CHUNK, LANE_CHUNK)
            part = ((std[rows, lanes].astype(F32) - center[:, lanes]) * scale[:, lanes]).astype(BF16)
            std[rows, lanes] = part
            value = value + jnp.dot(part, sketch[lanes, :], preferred_element_type=F32)
        keep_projection(r, value)
        return carry

    sketch_load.wait()
    lax.fori_loop(0, chunks, first_projection, 0)

    def group_lanes(yy, cc):
        return pl.ds(pl.multiple_of((yy * C + cc) * SNP_GROUP, SNP_GROUP), SNP_GROUP)

    def partial_group(yy, cc):
        value = jnp.dot(proj_t[...], std[:, group_lanes(yy, cc)], preferred_element_type=F32)
        for q in range(X):
            tot[yy, cc, q] = value[:, q * LANES:(q + 1) * LANES].reshape(8, 16, LANES)

    for it in range(ITERS):
        last = it + 1 == ITERS
        g_src[it] = dot_t(proj_t[...], proj_t[...]).reshape(C, X, 16, LANES)
        if it == 0:
            pl.semaphore_wait(barrier, len(others))
        gram_core = push(g_src.at[it, d], g_core.at[it], core_peer)

        core_sem = next(counter)
        for _ in range(Y - 1):
            next(counter)

        def core_copy(j, it=it, core_sem=core_sem):
            yy = lax.rem(y + 1 + j, Y)
            return describe(tot.at[yy, d], rxc.at[it, yy], core_sem + j, core_peer)

        def partial_other(j, carry):
            partial_group(lax.rem(y + 1 + j, Y), d)
            core_copy(j).start()
            return carry

        def partial_own(j, carry):
            partial_group(lax.rem(y + 1 + j, Y), c)
            return carry

        lax.fori_loop(0, 2, partial_other, 0)
        gram_core.wait_recv()
        g_half[it] = g_src[it, c] + g_core[it]
        gram_x = [push(g_half.at[it, xs[k]], g_rx.at[it, k - 1], x_peer[k]) for k in range(1, X)]
        lax.fori_loop(2, Y, partial_other, 0)
        lax.fori_loop(0, Y, partial_own, 0)
        for copy in gram_x:
            copy.wait_recv()
        g_y[it, y] = g_half[it, x] + g_rx[it, 0] + g_rx[it, 1] + g_rx[it, 2]
        gram_y = [push(g_y.at[it, y], g_y.at[it, y], y_peer[k]) for k in range(1, Y)]

        first_a, first_b = {}, {}
        for j in (1, 2, 3, 0):
            core_copy((j + 3) % 4).wait_recv()
            yy = ys[j]
            own[it, yy] = tot[yy, c] + rxc[it, yy]
            for k in range(1, X):
                first_a[j, k] = push(
                    own.at[it, yy, xs[k], pl.ds(0, 4)], rx1a.at[it, k - 1, yy], x_peer[k]
                )
            if j:
                for k in (1, 2, 3, 0):
                    first_b[k, j] = push(
                        own.at[it, yy, xs[k], pl.ds(4, 4)], rx1b.at[it, j - 1, xs[k]], y_peer[j]
                    )
        if last:
            keep_column = jnp.broadcast_to(keep_row.astype(F32), (LANES, keep_count)).T
            value = jnp.zeros((keep_count, LANES), F32)
            for q in range(std.shape[0] // LANES):
                hits = keep_column == (iota((keep_count, LANES), 1) + q * LANES).astype(F32)
                value = value + jnp.dot(
                    jnp.where(hits, 1.0, 0.0).astype(BF16), proj[q * LANES:(q + 1) * LANES, :],
                    preferred_element_type=F32,
                )
            kept_proj[...] = value
        for copy in gram_y:
            copy.wait_recv()
        g_z[it, z] = (g_y[it, 0] + g_y[it, 1]) + (g_y[it, 2] + g_y[it, 3])
        gram_z = [push(g_z.at[it, z], g_z.at[it, z], z_peer[k]) for k in range(1, Z)]

        second_a, second_b = [], []
        for j in (1, 2, 3, 0):
            for k in range(1, X):
                first_a[j, k].wait_recv()
            own[it, ys[j], x, 0:4] = (
                own[it, ys[j], x, 0:4] + rx1a[it, 0, ys[j]] + rx1a[it, 1, ys[j]] + rx1a[it, 2, ys[j]]
            )
            if j:
                second_a.append(push(own.at[it, ys[j], x, pl.ds(0, 4)], rx2a.at[it, j - 1], y_peer[j]))
            for k in range(1, Y):
                first_b[j, k].wait_recv()
            own[it, y, xs[j], 4:8] = (
                own[it, y, xs[j], 4:8] + rx1b[it, 0, xs[j]] + rx1b[it, 1, xs[j]] + rx1b[it, 2, xs[j]]
            )
            if j:
                second_b.append(push(own.at[it, y, xs[j], pl.ds(4, 4)], rx2b.at[it, j - 1], x_peer[j]))
        for copy in gram_z:
            copy.wait_recv()
        value = g_z[it, 0]
        for k in range(1, Z):
            value = value + g_z[it, k]
        g_x[it, x] = value
        gram_x = [push(g_x.at[it, x], g_x.at[it, x], x_peer[k]) for k in range(1, X)]
        for copy in second_a + second_b:
            copy.wait_recv()
        zsrc[it, 0:4] = own[it, y, x, 0:4] + rx2a[it, 0] + rx2a[it, 1] + rx2a[it, 2]
        zsrc[it, 4:8] = own[it, y, x, 4:8] + rx2b[it, 0] + rx2b[it, 1] + rx2b[it, 2]
        third = [push(zsrc.at[it, zs[k]], rxz.at[it, k - 1], z_peer[k]) for k in range(1, Z)]
        for copy in gram_x:
            copy.wait_recv()
        g_full[it, c] = g_x[it]
        gram_core = push(g_full.at[it, c], g_full.at[it, c], core_peer)
        for copy in third:
            copy.wait_recv()
        value = zsrc[it, z]
        for k in range(1, Z):
            value = value + rxz[it, k - 1]
        if last:
            mine = fin2.at[c, x]
        else:
            mine = fin.at[y, c, x]
        mine[z] = value
        gather_z = [push(mine.at[z], mine.at[z], z_peer[k]) for k in range(1, Z)]
        gram_core.wait_recv()
        gram[...] = g_full[it].reshape(LANES, LANES)
        panels = LANES // PIVOTS
        eliminate(gram, 0, 20)
        for copy in gather_z:
            copy.wait_recv()
        if last:
            gather_x = [push(mine, mine, x_peer[k]) for k in range(1, X)]
            gather_c = [push(mine, mine, core_peer)]
            for k in range(1, X):
                gather_x[k - 1].wait_recv()
                block = fin2.at[c, xs[X - k]]
                gather_c.append(push(block, block, core_peer))
            eliminate(gram, 20, panels)
            inverse[...] = finish_inverse(gram)
            scores[...] = dot_t(kept_proj[...], inverse[...], HIGHEST) * root
            results = [pltpu.make_async_copy(scores, scores_ref, out_sem.at[0])]
            results[0].start()

            def load_half(cc, place):
                value = jnp.concatenate([fin2[cc, q].reshape(LANES, LANES) for q in range(X)], axis=1)
                value = jnp.dot(inverse[...], value, precision=HIGHEST, preferred_element_type=F32)
                rows = pl.ds(pl.multiple_of(cc * SNP_GROUP, SNP_GROUP), SNP_GROUP)
                loads[rows, :] = value.T
                copy = pltpu.make_async_copy(loads.at[rows], loads_ref.at[rows], out_sem.at[place])
                copy.start()
                results.append(copy)

            load_half(c, 1)
            for copy in gather_c:
                copy.wait_recv()
            load_half(d, 2)
            for copy in results:
                copy.wait()
        else:
            half_a, half_b = pl.ds(0, 4), pl.ds(4, 4)

            def pass_on(block, half, peer):
                return push(block.at[half], block.at[half], peer)

            near_a = [pass_on(mine, half_a, y_peer[k]) for k in range(1, Y)]
            near_b = [pass_on(mine, half_b, x_peer[k]) for k in range(1, X)]
            late_a = [pass_on(mine, half_a, x_peer[k]) for k in range(1, X)]
            late_b = [pass_on(mine, half_b, y_peer[k]) for k in range(1, Y)]
            gather_c = [push(mine, mine, core_peer)]
            eliminate(gram, 20, panels)
            inverse[...] = finish_inverse(gram)
            corner_a, corner_b = {}, {}
            for j in range(1, Y):
                near_a[j - 1].wait_recv()
                for k in range(1, X):
                    corner_a[j, k] = pass_on(fin.at[ys[Y - j], c, x], half_a, x_peer[k])
                near_b[j - 1].wait_recv()
                for k in range(1, Y):
                    corner_b[j, k] = pass_on(fin.at[y, c, xs[X - j]], half_b, y_peer[k])
            acc[...] = jnp.zeros_like(acc)

            def add_group(yy, cc):
                value = jnp.concatenate([fin[yy, cc, q].reshape(LANES, LANES) for q in range(X)], axis=1)
                value = jnp.dot(inverse[...], value, precision=HIGHEST, preferred_element_type=F32)
                basis_t[...] = value.astype(BF16)

                def add_rows(r, carry):
                    rows = pl.ds(pl.multiple_of(r * HALF_ROWS, HALF_ROWS), HALF_ROWS)
                    acc[rows, :] = acc[rows, :] + dot_t(std[rows, group_lanes(yy, cc)], basis_t[...])
                    return carry

                lax.fori_loop(0, std.shape[0] // HALF_ROWS, add_rows, 0)

            same_y = [gather_c[0]]
            for j in range(1, X):
                late_a[j - 1].wait_recv()
                block = fin.at[y, c, xs[X - j]]
                same_y.append(push(block, block, core_peer))
            other_y = []
            for j in range(1, Y):
                late_b[j - 1].wait_recv()
                block = fin.at[ys[Y - j], c, x]
                other_y.append(push(block, block, core_peer))
            add_group(y, c)
            for copy in same_y:
                copy.wait_recv()
            add_group(y, d)
            for j in range(1, Y):
                for k in range(1, X):
                    corner_a[j, k].wait_recv()
                    corner_b[k, j].wait_recv()
                    block = fin.at[ys[Y - j], c, xs[X - k]]
                    other_y.append(push(block, block, core_peer))
                add_group(ys[Y - j], c)
            for copy in other_y:
                copy.wait_recv()

            def add_other(j, carry):
                add_group(lax.rem(y + j, Y), d)
                return carry

            lax.fori_loop(1, Y, add_other, 0)

            def keep_chunk(r, carry):
                rows = pl.ds(pl.multiple_of(r * ROW_CHUNK, ROW_CHUNK), ROW_CHUNK)
                keep_projection(r, acc[rows, :])
                return carry

            lax.fori_loop(0, chunks, keep_chunk, 0)
        for j in range(Y):
            core_copy(j).wait_send()
    for copy in sends:
        copy.wait_send()


def on_device(dosage, keep_rows, allele_counts, projection):
    groups = lax.axis_size("wide") * lax.axis_size("narrow")
    samples, snps = dosage.shape
    kept = keep_rows.shape[0]
    shares = snps // Y
    vmem = pl.BlockSpec(memory_space=pltpu.VMEM)
    piece = (4, 16, LANES)
    block = (8, 16, LANES)
    scratch = [
        ((samples, snps), BF16),
        ((snps, LANES), BF16),
        ((1, snps), F32),
        ((1, snps), F32),
        ((samples, LANES), F32),
        ((samples, LANES), BF16),
        ((LANES, samples), BF16),
        ((samples, LANES), F32),
        ((LANES, LANES), F32),
        ((LANES, LANES), F32),
        ((LANES, SNP_GROUP), BF16),
        ((kept, LANES), F32),
        ((shares, LANES), F32),
        ((kept, LANES), F32),
        ((Y, C, X) + block, F32),
        ((ITERS, Y, X) + block, F32),
        ((ITERS, Y, X) + block, F32),
        ((ITERS, X - 1, Y) + piece, F32),
        ((ITERS, Y - 1, X) + piece, F32),
        ((ITERS, Y - 1) + piece, F32),
        ((ITERS, X - 1) + piece, F32),
        ((ITERS,) + block, F32),
        ((ITERS, Z - 1, 16, LANES), F32),
        ((Y, C, X) + block, F32),
        ((C, X) + block, F32),
        ((ITERS, C, X, 16, LANES), F32),
        ((ITERS, X, 16, LANES), F32),
        ((ITERS, X, 16, LANES), F32),
        ((ITERS, X - 1, 16, LANES), F32),
        ((ITERS, Y, 16, LANES), F32),
        ((ITERS, Z, 16, LANES), F32),
        ((ITERS, X, 16, LANES), F32),
        ((ITERS, C, X, 16, LANES), F32),
    ]
    any_place = pl.BlockSpec(memory_space=pl.ANY)
    results = (
        jax.ShapeDtypeStruct((kept, LANES), F32),
        jax.ShapeDtypeStruct((shares, LANES), F32),
    )
    computed = pl.pallas_call(
        functools.partial(kernel, samples * groups, math.sqrt(kept * groups)),
        name="subspace",
        out_shape=results,
        in_specs=[any_place, vmem, vmem, any_place],
        out_specs=(any_place, any_place),
        scratch_shapes=[pltpu.VMEM(shape, kind) for shape, kind in scratch]
        + [
            pltpu.SemaphoreType.DMA((samples // ROW_CHUNK,)),
            pltpu.SemaphoreType.DMA,
            pltpu.SemaphoreType.DMA((3,)),
            pltpu.SemaphoreType.DMA((220,)),
            pltpu.SemaphoreType.DMA((220,)),
        ],
        compiler_params=pltpu.CompilerParams(
            collective_id=0, has_side_effects=True, vmem_limit_bytes=56 * 2**20
        ),
        cost_estimate=pl.CostEstimate(flops=4_500_000_000, bytes_accessed=12_000_000, transcendentals=0),
    )(dosage, keep_rows.reshape(kept // LANES, LANES), allele_counts.reshape(1, snps), projection)
    return pl.pallas_call(
        hand_on,
        name="outputs",
        out_shape=results,
        in_specs=[any_place, any_place],
        out_specs=(any_place, any_place),
        scratch_shapes=[
            pltpu.VMEM((kept, LANES), F32),
            pltpu.VMEM((shares, LANES), F32),
            pltpu.SemaphoreType.DMA((4 * PARTS,)),
        ],
        compiler_params=pltpu.CompilerParams(vmem_limit_bytes=56 * 2**20),
        cost_estimate=pl.CostEstimate(flops=0, bytes_accessed=2_000_000, transcendentals=0),
    )(*computed)


def solution(mesh):
    in_specs = (P(("wide", "narrow"), None), P(("wide", "narrow")), P(), P())
    out_specs = (P(("wide", "narrow"), None), P("narrow", None))
    return jax.shard_map(
        on_device, mesh=mesh, in_specs=in_specs, out_specs=out_specs, check_vma=False
    )
```

```python
import functools
import itertools
import math

import jax
import jax.numpy as jnp
from jax import lax
from jax.experimental import pallas as pl
from jax.experimental.pallas import tpu as pltpu
from jax.sharding import PartitionSpec as P

X, Y, Z, C = 4, 4, 8, 2
LANES = 128
SNP_GROUP = 4 * LANES
ROW_CHUNK = 256
HALF_ROWS = 512
LANE_CHUNK = 1024
PIVOTS = 4
ITERS = 2
PARTS = 2
MESH = pl.DeviceIdType.MESH
HIGHEST = lax.Precision.HIGHEST
F32 = jnp.float32
BF16 = jnp.bfloat16


def device_at(x, y, z, c):
    return ((x * Z + z) * C + c, y)


def iota(shape, dim):
    return lax.broadcasted_iota(jnp.int32, shape, dim)


def dot_t(left, right, precision=None):
    return lax.dot_general(
        left, right, (((1,), (1,)), ((), ())), precision=precision, preferred_element_type=F32
    )


def eliminate(work, first, last):
    n = work.shape[0]
    row = iota((n, 1), 0)
    lane = iota((n, n), 1)
    lane1 = iota((1, n), 1)

    def panel(step, carry):
        k = step * PIVOTS
        whole = work[...]
        rows = [work[pl.ds(k + i, 1), :] for i in range(PIVOTS)]
        entry = {
            (i, l): jnp.sum(jnp.where(lane1 == k + l, rows[i], 0.0), axis=1, keepdims=True)
            for i in range(PIVOTS)
            for l in range(i, PIVOTS)
        }
        columns = [
            jnp.sum(jnp.where(lane == k + l, whole, 0.0), axis=1, keepdims=True)
            for l in range(PIVOTS)
        ]
        total = jnp.where((lane >= k) & (lane < k + PIVOTS) & (row >= k + PIVOTS), 0.0, whole)
        factors = []
        for j in range(PIVOTS):
            turn = 1.0 / entry[j, j]
            factor = jnp.where(row > k + j, columns[j] * turn, 0.0)
            factors.append(factor)
            own = jnp.where(lane1 == k + j, 1.0, rows[j])
            for l in range(j + 1, PIVOTS):
                columns[l] = columns[l] - factor * entry[j, l]
                less = entry[j, l] * turn
                rows[l] = jnp.where(lane1 == k + j, 0.0, rows[l]) - less * own
                for later in range(l, PIVOTS):
                    entry[l, later] = entry[l, later] - less * entry[j, later]
        for j in range(PIVOTS):
            own = jnp.where(lane1 == k + j, 1.0, rows[j])
            own = jnp.where((lane1 > k + j) & (lane1 < k + PIVOTS), 0.0, own)
            total = total - factors[j] * own
        work[...] = total
        for j in range(PIVOTS):
            work[pl.ds(k + j, 1), :] = rows[j]
        return carry

    lax.fori_loop(first, last, panel, 0)


def finish_inverse(work):
    n = work.shape[0]
    whole = work[...]
    row, lane = iota((n, n), 0), iota((n, n), 1)
    pivot = jnp.sum(jnp.where(row == lane, whole, 0.0), axis=1, keepdims=True)
    unit = jnp.where(lane < row, whole, jnp.where(lane == row, 1.0, 0.0))
    return unit * (1.0 / jnp.sqrt(pivot))


def hand_on(scores_in, loads_in, scores_out, loads_out, scores, loads, sem):
    parts = []
    for source, held, target in ((scores_in, scores, scores_out), (loads_in, loads, loads_out)):
        size = source.shape[0] // PARTS
        for q in range(PARTS):
            rows, n = pl.ds(q * size, size), len(parts)
            parts.append((
                pltpu.make_async_copy(source.at[rows], held.at[rows], sem.at[n]),
                pltpu.make_async_copy(held.at[rows], target.at[rows], sem.at[n + 2 * PARTS]),
            ))
    for read, _ in parts:
        read.start()
    for read, write in parts:
        read.wait()
        write.start()
    for _, write in parts:
        write.wait()


def kernel(
    samples_total, root,
    dose_ref, keep_ref, counts_ref, sketch_ref,
    scores_ref, loads_ref,
    std, sketch, center, scale, mask, proj, proj_t, acc, gram, inverse, basis_t, scores, loads, kept_proj,
    tot, rxc, own, rx1a, rx1b, rx2a, rx2b, zsrc, rxz, fin, fin2,
    g_src, g_core, g_half, g_rx, g_y, g_z, g_x, g_full,
    load_sem, sketch_sem, out_sem, send_sem, recv_sem,
):
    wide = lax.axis_index("wide")
    y = lax.axis_index("narrow")
    x, z, c = wide // (Z * C), lax.rem(wide // C, Z), lax.rem(wide, C)
    d = 1 - c
    xs = [lax.rem(x + k, X) for k in range(X)]
    ys = [lax.rem(y + k, Y) for k in range(Y)]
    zs = [lax.rem(z + k, Z) for k in range(Z)]
    core_peer = device_at(x, y, z, d)
    x_peer = [device_at(v, y, z, c) for v in xs]
    y_peer = [device_at(x, v, z, c) for v in ys]
    z_peer = [device_at(x, y, v, c) for v in zs]
    chunks = std.shape[0] // ROW_CHUNK
    snps = std.shape[1]

    def load(r):
        rows = pl.ds(r * ROW_CHUNK, ROW_CHUNK)
        return pltpu.make_async_copy(dose_ref.at[rows], std.at[rows], load_sem.at[r])

    sketch_load = pltpu.make_async_copy(sketch_ref, sketch, sketch_sem)
    sketch_load.start()
    for r in range(chunks):
        load(r).start()
    barrier = pltpu.get_barrier_semaphore()
    far = sorted(range(1, Z), key=lambda k: -min(k, Z - k))
    others = [core_peer] + x_peer[1:] + y_peer[1:] + z_peer[1:]
    for other in others:
        pl.semaphore_signal(barrier, inc=1, device_id=other, device_id_type=MESH)

    counter = itertools.count()
    sends = []

    def describe(src, dst, sem, peer):
        return pltpu.make_async_remote_copy(
            src_ref=src, dst_ref=dst, send_sem=send_sem.at[sem], recv_sem=recv_sem.at[sem],
            device_id=peer, device_id_type=MESH,
        )

    def push(src, dst, peer):
        copy = describe(src, dst, next(counter), peer)
        copy.start()
        sends.append(copy)
        return copy

    frequency = counts_ref[...].astype(F32) / (2.0 * samples_total)
    center[...] = 2.0 * frequency
    scale[...] = 1.0 / jnp.sqrt(2.0 * frequency * (1.0 - frequency))
    keep_row = jnp.concatenate([keep_ref[q:q + 1, :] for q in range(keep_ref.shape[0])], axis=1)
    keep_count = keep_row.shape[1]
    ones = jnp.ones((keep_count, LANES), BF16)

    def mark(r, carry):
        hits = iota((ROW_CHUNK, keep_count), 0) + r * ROW_CHUNK == keep_row
        mask[pl.ds(pl.multiple_of(r * ROW_CHUNK, ROW_CHUNK), ROW_CHUNK), :] = jnp.dot(
            jnp.where(hits, 1.0, 0.0).astype(BF16), ones, preferred_element_type=F32
        )
        return carry

    lax.fori_loop(0, chunks, mark, 0)

    def keep_projection(r, value):
        rows = pl.ds(pl.multiple_of(r * ROW_CHUNK, ROW_CHUNK), ROW_CHUNK)
        value = value.astype(BF16).astype(F32) * mask[rows, :]
        proj[rows, :] = value.astype(BF16)
        proj_t[:, rows] = value.T.astype(BF16)

    def first_projection(r, carry):
        load(r).wait()
        rows = pl.ds(pl.multiple_of(r * ROW_CHUNK, ROW_CHUNK), ROW_CHUNK)
        value = jnp.zeros((ROW_CHUNK, LANES), F32)
        for q in range(snps // LANE_CHUNK):
            lanes = pl.ds(q * LANE_CHUNK, LANE_CHUNK)
            part = ((std[rows, lanes].astype(F32) - center[:, lanes]) * scale[:, lanes]).astype(BF16)
            std[rows, lanes] = part
            value = value + jnp.dot(part, sketch[lanes, :], preferred_element_type=F32)
        keep_projection(r, value)
        return carry

    sketch_load.wait()
    lax.fori_loop(0, chunks, first_projection, 0)

    def group_lanes(yy, cc):
        return pl.ds(pl.multiple_of((yy * C + cc) * SNP_GROUP, SNP_GROUP), SNP_GROUP)

    def partial_group(yy, cc):
        value = jnp.dot(proj_t[...], std[:, group_lanes(yy, cc)], preferred_element_type=F32)
        for q in range(X):
            tot[yy, cc, q] = value[:, q * LANES:(q + 1) * LANES].reshape(8, 16, LANES)

    for it in range(ITERS):
        last = it + 1 == ITERS
        g_src[it] = dot_t(proj_t[...], proj_t[...]).reshape(C, X, 16, LANES)
        if it == 0:
            pl.semaphore_wait(barrier, len(others))
        gram_core = push(g_src.at[it, d], g_core.at[it], core_peer)

        core_sem = next(counter)
        for _ in range(Y - 1):
            next(counter)

        def core_copy(j, it=it, core_sem=core_sem):
            yy = lax.rem(y + 1 + j, Y)
            return describe(tot.at[yy, d], rxc.at[it, yy], core_sem + j, core_peer)

        def partial_other(j, carry):
            partial_group(lax.rem(y + 1 + j, Y), d)
            core_copy(j).start()
            return carry

        def partial_own(j, carry):
            partial_group(lax.rem(y + 1 + j, Y), c)
            return carry

        lax.fori_loop(0, 2, partial_other, 0)
        gram_core.wait_recv()
        g_half[it] = g_src[it, c] + g_core[it]
        gram_x = [push(g_half.at[it, xs[k]], g_rx.at[it, k - 1], x_peer[k]) for k in range(1, X)]
        lax.fori_loop(2, Y, partial_other, 0)
        lax.fori_loop(0, Y, partial_own, 0)
        for copy in gram_x:
            copy.wait_recv()
        g_y[it, y] = g_half[it, x] + g_rx[it, 0] + g_rx[it, 1] + g_rx[it, 2]
        gram_y = [push(g_y.at[it, y], g_y.at[it, y], y_peer[k]) for k in range(1, Y)]

        first_a, first_b = {}, {}
        for j in (1, 2, 3, 0):
            core_copy((j + 3) % 4).wait_recv()
            yy = ys[j]
            own[it, yy] = tot[yy, c] + rxc[it, yy]
            for k in range(1, X):
                first_a[j, k] = push(
                    own.at[it, yy, xs[k], pl.ds(0, 4)], rx1a.at[it, k - 1, yy], x_peer[k]
                )
            if j:
                for k in (1, 2, 3, 0):
                    first_b[k, j] = push(
                        own.at[it, yy, xs[k], pl.ds(4, 4)], rx1b.at[it, j - 1, xs[k]], y_peer[j]
                    )
        if last:
            keep_column = jnp.broadcast_to(keep_row.astype(F32), (LANES, keep_count)).T
            value = jnp.zeros((keep_count, LANES), F32)
            for q in range(std.shape[0] // LANES):
                hits = keep_column == (iota((keep_count, LANES), 1) + q * LANES).astype(F32)
                value = value + jnp.dot(
                    jnp.where(hits, 1.0, 0.0).astype(BF16), proj[q * LANES:(q + 1) * LANES, :],
                    preferred_element_type=F32,
                )
            kept_proj[...] = value
        for copy in gram_y:
            copy.wait_recv()
        g_z[it, z] = (g_y[it, 0] + g_y[it, 1]) + (g_y[it, 2] + g_y[it, 3])
        gram_z = [push(g_z.at[it, z], g_z.at[it, z], z_peer[k]) for k in far]

        second_a, second_b = [], []
        for j in (1, 2, 3, 0):
            for k in range(1, X):
                first_a[j, k].wait_recv()
            own[it, ys[j], x, 0:4] = (
                own[it, ys[j], x, 0:4] + rx1a[it, 0, ys[j]] + rx1a[it, 1, ys[j]] + rx1a[it, 2, ys[j]]
            )
            if j:
                second_a.append(push(own.at[it, ys[j], x, pl.ds(0, 4)], rx2a.at[it, j - 1], y_peer[j]))
            for k in range(1, Y):
                first_b[j, k].wait_recv()
            own[it, y, xs[j], 4:8] = (
                own[it, y, xs[j], 4:8] + rx1b[it, 0, xs[j]] + rx1b[it, 1, xs[j]] + rx1b[it, 2, xs[j]]
            )
            if j:
                second_b.append(push(own.at[it, y, xs[j], pl.ds(4, 4)], rx2b.at[it, j - 1], x_peer[j]))
        for copy in gram_z:
            copy.wait_recv()
        value = g_z[it, 0]
        for k in range(1, Z):
            value = value + g_z[it, k]
        g_x[it, x] = value
        gram_x = [push(g_x.at[it, x], g_x.at[it, x], x_peer[k]) for k in range(1, X)]
        for copy in second_a + second_b:
            copy.wait_recv()
        zsrc[it, 0:4] = own[it, y, x, 0:4] + rx2a[it, 0] + rx2a[it, 1] + rx2a[it, 2]
        zsrc[it, 4:8] = own[it, y, x, 4:8] + rx2b[it, 0] + rx2b[it, 1] + rx2b[it, 2]
        third = [push(zsrc.at[it, zs[k]], rxz.at[it, k - 1], z_peer[k]) for k in far]
        for copy in gram_x:
            copy.wait_recv()
        g_full[it, c] = g_x[it]
        gram_core = push(g_full.at[it, c], g_full.at[it, c], core_peer)
        for copy in third:
            copy.wait_recv()
        value = zsrc[it, z]
        for k in range(1, Z):
            value = value + rxz[it, k - 1]
        if last:
            mine = fin2.at[c, x]
        else:
            mine = fin.at[y, c, x]
        mine[z] = value
        gather_z = [push(mine.at[z], mine.at[z], z_peer[k]) for k in far]
        gram_core.wait_recv()
        gram[...] = g_full[it].reshape(LANES, LANES)
        panels = LANES // PIVOTS
        eliminate(gram, 0, 20)
        for copy in gather_z:
            copy.wait_recv()
        if last:
            gather_x = [push(mine, mine, x_peer[k]) for k in range(1, X)]
            gather_c = [push(mine, mine, core_peer)]
            for k in range(1, X):
                gather_x[k - 1].wait_recv()
                block = fin2.at[c, xs[X - k]]
                gather_c.append(push(block, block, core_peer))
            eliminate(gram, 20, panels)
            inverse[...] = finish_inverse(gram)
            scores[...] = dot_t(kept_proj[...], inverse[...], HIGHEST) * root
            results = [pltpu.make_async_copy(scores, scores_ref, out_sem.at[0])]
            results[0].start()

            def load_half(cc, place):
                value = jnp.concatenate([fin2[cc, q].reshape(LANES, LANES) for q in range(X)], axis=1)
                value = jnp.dot(inverse[...], value, precision=HIGHEST, preferred_element_type=F32)
                rows = pl.ds(pl.multiple_of(cc * SNP_GROUP, SNP_GROUP), SNP_GROUP)
                loads[rows, :] = value.T
                copy = pltpu.make_async_copy(loads.at[rows], loads_ref.at[rows], out_sem.at[place])
                copy.start()
                results.append(copy)

            load_half(c, 1)
            for copy in gather_c:
                copy.wait_recv()
            load_half(d, 2)
            for copy in results:
                copy.wait()
        else:
            half_a, half_b = pl.ds(0, 4), pl.ds(4, 4)

            def pass_on(block, half, peer):
                return push(block.at[half], block.at[half], peer)

            near_a = [pass_on(mine, half_a, y_peer[k]) for k in range(1, Y)]
            near_b = [pass_on(mine, half_b, x_peer[k]) for k in range(1, X)]
            late_a = [pass_on(mine, half_a, x_peer[k]) for k in range(1, X)]
            late_b = [pass_on(mine, half_b, y_peer[k]) for k in range(1, Y)]
            gather_c = [push(mine, mine, core_peer)]
            eliminate(gram, 20, panels)
            inverse[...] = finish_inverse(gram)
            corner_a, corner_b = {}, {}
            for j in range(1, Y):
                near_a[j - 1].wait_recv()
                for k in range(1, X):
                    corner_a[j, k] = pass_on(fin.at[ys[Y - j], c, x], half_a, x_peer[k])
                near_b[j - 1].wait_recv()
                for k in range(1, Y):
                    corner_b[j, k] = pass_on(fin.at[y, c, xs[X - j]], half_b, y_peer[k])
            acc[...] = jnp.zeros_like(acc)

            def add_group(yy, cc):
                value = jnp.concatenate([fin[yy, cc, q].reshape(LANES, LANES) for q in range(X)], axis=1)
                value = jnp.dot(inverse[...], value, precision=HIGHEST, preferred_element_type=F32)
                basis_t[...] = value.astype(BF16)

                def add_rows(r, carry):
                    rows = pl.ds(pl.multiple_of(r * HALF_ROWS, HALF_ROWS), HALF_ROWS)
                    acc[rows, :] = acc[rows, :] + dot_t(std[rows, group_lanes(yy, cc)], basis_t[...])
                    return carry

                lax.fori_loop(0, std.shape[0] // HALF_ROWS, add_rows, 0)

            same_y = [gather_c[0]]
            for j in range(1, X):
                late_a[j - 1].wait_recv()
                block = fin.at[y, c, xs[X - j]]
                same_y.append(push(block, block, core_peer))
            other_y = []
            for j in range(1, Y):
                late_b[j - 1].wait_recv()
                block = fin.at[ys[Y - j], c, x]
                other_y.append(push(block, block, core_peer))
            add_group(y, c)
            for copy in same_y:
                copy.wait_recv()
            add_group(y, d)
            for j in range(1, Y):
                for k in range(1, X):
                    corner_a[j, k].wait_recv()
                    corner_b[k, j].wait_recv()
                    block = fin.at[ys[Y - j], c, xs[X - k]]
                    other_y.append(push(block, block, core_peer))
                add_group(ys[Y - j], c)
            for copy in other_y:
                copy.wait_recv()

            def add_other(j, carry):
                add_group(lax.rem(y + j, Y), d)
                return carry

            lax.fori_loop(1, Y, add_other, 0)

            def keep_chunk(r, carry):
                rows = pl.ds(pl.multiple_of(r * ROW_CHUNK, ROW_CHUNK), ROW_CHUNK)
                keep_projection(r, acc[rows, :])
                return carry

            lax.fori_loop(0, chunks, keep_chunk, 0)
        for j in range(Y):
            core_copy(j).wait_send()
    for copy in sends:
        copy.wait_send()


def on_device(dosage, keep_rows, allele_counts, projection):
    groups = lax.axis_size("wide") * lax.axis_size("narrow")
    samples, snps = dosage.shape
    kept = keep_rows.shape[0]
    shares = snps // Y
    vmem = pl.BlockSpec(memory_space=pltpu.VMEM)
    piece = (4, 16, LANES)
    block = (8, 16, LANES)
    scratch = [
        ((samples, snps), BF16),
        ((snps, LANES), BF16),
        ((1, snps), F32),
        ((1, snps), F32),
        ((samples, LANES), F32),
        ((samples, LANES), BF16),
        ((LANES, samples), BF16),
        ((samples, LANES), F32),
        ((LANES, LANES), F32),
        ((LANES, LANES), F32),
        ((LANES, SNP_GROUP), BF16),
        ((kept, LANES), F32),
        ((shares, LANES), F32),
        ((kept, LANES), F32),
        ((Y, C, X) + block, F32),
        ((ITERS, Y, X) + block, F32),
        ((ITERS, Y, X) + block, F32),
        ((ITERS, X - 1, Y) + piece, F32),
        ((ITERS, Y - 1, X) + piece, F32),
        ((ITERS, Y - 1) + piece, F32),
        ((ITERS, X - 1) + piece, F32),
        ((ITERS,) + block, F32),
        ((ITERS, Z - 1, 16, LANES), F32),
        ((Y, C, X) + block, F32),
        ((C, X) + block, F32),
        ((ITERS, C, X, 16, LANES), F32),
        ((ITERS, X, 16, LANES), F32),
        ((ITERS, X, 16, LANES), F32),
        ((ITERS, X - 1, 16, LANES), F32),
        ((ITERS, Y, 16, LANES), F32),
        ((ITERS, Z, 16, LANES), F32),
        ((ITERS, X, 16, LANES), F32),
        ((ITERS, C, X, 16, LANES), F32),
    ]
    any_place = pl.BlockSpec(memory_space=pl.ANY)
    results = (
        jax.ShapeDtypeStruct((kept, LANES), F32),
        jax.ShapeDtypeStruct((shares, LANES), F32),
    )
    computed = pl.pallas_call(
        functools.partial(kernel, samples * groups, math.sqrt(kept * groups)),
        name="subspace",
        out_shape=results,
        in_specs=[any_place, vmem, vmem, any_place],
        out_specs=(any_place, any_place),
        scratch_shapes=[pltpu.VMEM(shape, kind) for shape, kind in scratch]
        + [
            pltpu.SemaphoreType.DMA((samples // ROW_CHUNK,)),
            pltpu.SemaphoreType.DMA,
            pltpu.SemaphoreType.DMA((3,)),
            pltpu.SemaphoreType.DMA((220,)),
            pltpu.SemaphoreType.DMA((220,)),
        ],
        compiler_params=pltpu.CompilerParams(
            collective_id=0, has_side_effects=True, vmem_limit_bytes=56 * 2**20
        ),
        cost_estimate=pl.CostEstimate(flops=4_500_000_000, bytes_accessed=12_000_000, transcendentals=0),
    )(dosage, keep_rows.reshape(kept // LANES, LANES), allele_counts.reshape(1, snps), projection)
    return pl.pallas_call(
        hand_on,
        name="outputs",
        out_shape=results,
        in_specs=[any_place, any_place],
        out_specs=(any_place, any_place),
        scratch_shapes=[
            pltpu.VMEM((kept, LANES), F32),
            pltpu.VMEM((shares, LANES), F32),
            pltpu.SemaphoreType.DMA((4 * PARTS,)),
        ],
        compiler_params=pltpu.CompilerParams(vmem_limit_bytes=56 * 2**20),
        cost_estimate=pl.CostEstimate(flops=0, bytes_accessed=2_000_000, transcendentals=0),
    )(*computed)


def solution(mesh):
    in_specs = (P(("wide", "narrow"), None), P(("wide", "narrow")), P(), P())
    out_specs = (P(("wide", "narrow"), None), P("narrow", None))
    return jax.shard_map(
        on_device, mesh=mesh, in_specs=in_specs, out_specs=out_specs, check_vma=False
    )
```
